32 devices in a mesh: shard: 2 (over y), ctx: 4 (over z), tp: 4 (over x, core).
Axes of the slice: x: 2, y: 2, z: 4, core: 2. Of those that a mesh axis runs over, the one named last changes fastest.
Arguments:
- tokens: bfloat16 [2, 2048, 768], P('shard', 'ctx'), may hold values from -6 to 6
- segments: int32 [2, 2048], P('shard', 'ctx'), may hold values from 0 to 8, as said below
- gain_one: bfloat16 [768], P(('shard', 'ctx')), may hold values from 0.5 to 1.5
- shift_one: bfloat16 [768], P(('shard', 'ctx')), may hold values from -4 to 4
- qkv_weight: bfloat16 [768, 12, 192], P(('shard', 'ctx'), 'tp'), may hold values from -0.21875 to 0.21875
- qv_bias: bfloat16 [12, 128], P('tp', ('shard', 'ctx')), may hold values from -3 to 3
- proj_weight: bfloat16 [12, 64, 768], P('tp', None, ('shard', 'ctx')), may hold values from -0.875 to 0.875
- proj_bias: bfloat16 [768], P(('shard', 'ctx')), may hold values from -6 to 6
- gain_two: bfloat16 [768], P(('shard', 'ctx')), may hold values from 0.5 to 1.5
- shift_two: bfloat16 [768], P(('shard', 'ctx')), may hold values from -4 to 4
- up_weight: bfloat16 [768, 3072], P(('shard', 'ctx'), 'tp'), may hold values from -0.21875 to 0.21875
- up_bias: bfloat16 [24, 128], P('tp', ('shard', 'ctx')), may hold values from -6 to 6
- down_weight: bfloat16 [3072, 768], P('tp', ('shard', 'ctx')), may hold values from -0.109375 to 0.109375
- down_bias: bfloat16 [768], P(('shard', 'ctx')), may hold values from -6 to 6
- cotangent: bfloat16 [2, 2048, 768], P('shard', 'ctx'), may hold values from -6 to 6
Outputs:
- layer_out: bfloat16 [2, 2048, 768], P('shard', 'ctx')
- input_grad: float32 [2, 2048, 768], P('shard', 'ctx')
- gain_one_grad: float32 [768], P(('shard', 'ctx'))
- shift_one_grad: float32 [768], P(('shard', 'ctx'))
- qkv_grad: float32 [768, 12, 192], P(('shard', 'ctx'), 'tp')
- qv_bias_grad: float32 [12, 128], P('tp', ('shard', 'ctx'))
- proj_grad: float32 [12, 64, 768], P('tp', None, ('shard', 'ctx'))
- proj_bias_grad: float32 [768], P(('shard', 'ctx'))
- gain_two_grad: float32 [768], P(('shard', 'ctx'))
- shift_two_grad: float32 [768], P(('shard', 'ctx'))
- up_grad: float32 [768, 3072], P(('shard', 'ctx'), 'tp')
- up_bias_grad: float32 [24, 128], P('tp', ('shard', 'ctx'))
- down_grad: float32 [3072, 768], P('tp', ('shard', 'ctx'))
- down_bias_grad: float32 [768], P(('shard', 'ctx'))
The draws below stay inside these ranges and needn't reach their ends.
Inputs may be any that keep to these rules, and one draw needn't show every extreme that they name: `segments`: document numbers never fall along a sequence; in every sequence one document starts within the first 512 tokens and ends within the last 512.
All inputs are finite; a program needn't handle non-finite values.
Results may differ from the reference program's by a relative error of at most 0.03.
Values may be sent and summed in bfloat16 or wider, within the bound.
A program may use at most 128 MiB of HBM per device.

```python
import math
import jax
import jax.numpy as jnp
from jax import lax

D = 768
H = 12
HD = 64
FF = 3072
BLK = 512
SEQ = 2048
SEQS = 2


def draw_segments(key, part):
    key = jax.random.fold_in(key, 11)

    def one_row(row_key):
        parts = jax.random.split(row_key, 4)
        begin = jax.random.randint(parts[0], (), 1, BLK, dtype=jnp.int32)
        finish = jax.random.randint(parts[1], (), SEQ - BLK + 1, SEQ, dtype=jnp.int32)
        early = jnp.minimum(jax.random.randint(parts[2], (3,), 1, BLK, dtype=jnp.int32), begin)
        late = jnp.maximum(jax.random.randint(parts[3], (3,), SEQ - BLK + 1, SEQ, dtype=jnp.int32), finish)
        cuts = jnp.concatenate([begin[None], finish[None], early, late])
        places = jnp.arange(SEQ, dtype=jnp.int32)
        return jnp.sum((places[:, None] >= cuts[None, :]).astype(jnp.int32), axis=1)
    return jax.vmap(one_row)(jax.random.split(key, SEQS))


def with_spikes(array, key, source, target, blocks, factor):
    def block_of(axis_at):
        return (jnp.arange(array.shape[axis_at]) // (array.shape[axis_at] // blocks)).reshape((-1,) + (1,) * (array.ndim - 1 - axis_at))

    near = jax.random.permutation(key, blocks)[block_of(target)]
    far = (block_of(target) + blocks // 2) % blocks
    return jnp.where((block_of(source) == near) | (block_of(source) == far), factor * array, array)


def steps_of(own_key, dims, pieces, low, largest):
    factor_of = 1.0
    for axis_at, blocks in pieces:
        draws = jax.random.uniform(jax.random.fold_in(jax.random.fold_in(own_key, 6), axis_at), (blocks,), jnp.float32, low / len(pieces), largest / len(pieces))
        factor_of = factor_of * jnp.repeat(jnp.exp(draws), dims[axis_at] // blocks).reshape((-1,) + (1,) * (len(dims) - 1 - axis_at))
    return factor_of


def bell_draw(key, dims, scale, bound, shards=(), kind=jnp.bfloat16):
    drawn = jax.random.normal(key, dims, jnp.float32) * scale
    if len(shards) > 0:
        drawn = steps_of(key, dims, shards, -0.22, 0.18) * drawn
    return jnp.clip(drawn, min=-bound, max=bound).astype(kind)


def bell_draw_with(rng, shape, scale, reach, shards, heavy, kind=jnp.bfloat16):
    values = scale * jax.random.normal(rng, shape, jnp.float32)
    if shards:
        values = values * steps_of(rng, shape, shards, -0.22, 0.18)
    return jnp.clip(with_spikes(values, jax.random.fold_in(rng, 3), *heavy), -reach, reach).astype(kind)


def setup_inputs(seed: int = 0) -> dict:
    seeds = jax.random.split(jax.random.key(seed), 16)
    return {
        "tokens": bell_draw(seeds[0], (SEQS, SEQ, D), 1.0, 6.0, ((0, 2), (1, 4))),
        "segments": draw_segments(jax.random.fold_in(seeds[15], 71), 0),
        "gain_one": jnp.clip(1.0 + 0.1 * jax.random.normal(seeds[2], (D,), jnp.float32), 0.5, 1.5).astype(jnp.bfloat16),
        "shift_one": bell_draw(seeds[3], (D,), 0.3, 4.0, ((0, 8),)),
        "qkv_weight": bell_draw(seeds[4], (D, H, 3 * HD), D ** -0.5, 0.21875, ((0, 8), (1, 4))),
        "qv_bias": bell_draw(seeds[5], (H, 2 * HD), 0.2, 3.0, ((0, 4), (1, 8))),
        "proj_weight": bell_draw(seeds[6], (H, HD, D), (D // 16) ** -0.5, 0.875, ((0, 4), (2, 8))),
        "proj_bias": bell_draw(seeds[7], (D,), 0.5, 6.0, ((0, 8),)),
        "gain_two": jnp.clip(1.0 + 0.1 * jax.random.normal(seeds[8], (D,), jnp.float32), 0.5, 1.5).astype(jnp.bfloat16),
        "shift_two": bell_draw(seeds[9], (D,), 0.3, 4.0, ((0, 8),)),
        "up_weight": bell_draw(seeds[10], (D, FF), D ** -0.5, 0.21875, ((0, 8), (1, 4))),
        "up_bias": bell_draw(seeds[11], (FF // 128, 128), 0.5, 6.0, ((0, 4), (1, 8))),
        "down_weight": bell_draw(seeds[12], (FF, D), FF ** -0.5, 0.109375, ((0, 4), (1, 8))),
        "down_bias": bell_draw(seeds[13], (D,), 0.5, 6.0, ((0, 8),)),
        "cotangent": bell_draw_with(seeds[14], (SEQS, SEQ, D), 1.0, 6.0, ((0, 2), (1, 4)), (1, 2, 4, 2.0)),
    }


HIGH = lax.Precision.HIGHEST
eps_norm = 1e-05
masked_value = -1e+30
gelu_coeff = 0.7978845608028654

@jax.custom_vjp
def low(v):
    return lax.optimization_barrier(v.astype(jnp.bfloat16)).astype(jnp.float32)

@jax.custom_vjp
def low_back(v):
    return v

def low_keep(v):
    return (low(v), None)

def low_pass(kept, grad):
    return (grad,)

def back_keep(v):
    return (v, None)

def back_low(kept, grad):
    return (low(grad),)
low.defvjp(low_keep, low_pass)
low_back.defvjp(back_keep, back_low)

def mat(left, right):
    return jnp.dot(left, right, precision=HIGH, preferred_element_type=jnp.float32)

def layer_norm(values, gain, shift):
    center = values - lax.optimization_barrier(jnp.mean(values, axis=-1, keepdims=True))
    spread = lax.optimization_barrier(jnp.mean(center * center, axis=-1, keepdims=True))
    return center * lax.rsqrt(spread + eps_norm) * gain + shift

def gelu_tanh(values):
    return 0.5 * values * (1.0 + jnp.tanh(gelu_coeff * (values + 0.044715 * values * values * values)))

def layer(seq_tokens, seq_segments, gain_one, shift_one, qkv_weight, qv_bias, proj_weight, proj_bias, gain_two, shift_two, up_weight, up_bias, down_weight, down_bias):
    length = seq_tokens.shape[0]
    model = seq_tokens.shape[1]
    heads = qkv_weight.shape[1]
    width = qkv_weight.shape[2] // 3
    scale = width ** (-0.5)
    normed = low(layer_norm(seq_tokens, gain_one, shift_one))
    projected = mat(normed, qkv_weight.reshape(model, heads * 3 * width)).reshape(length, heads, 3 * width)
    query = low(low_back(projected[:, :, :width] + qv_bias[:, :width]))
    keys = low(low_back(projected[:, :, width:2 * width]))
    values = low(low_back(projected[:, :, 2 * width:] + qv_bias[:, width:]))
    block = math.gcd(length, 512)
    positions = jnp.arange(length, dtype=jnp.int32)

    def attend(index):
        start = (index * block).astype(jnp.int32)
        query_rows = lax.dynamic_slice_in_dim(query, start, block, 0)
        query_seg = lax.dynamic_slice_in_dim(seq_segments, start, block, 0)
        query_pos = start + jnp.arange(block, dtype=jnp.int32)
        scores = low_back(jnp.einsum('qhd,khd->hqk', query_rows, keys, precision=HIGH) * scale)
        allowed = (positions[None, :] <= query_pos[:, None]) & (seq_segments[None, :] == query_seg[:, None])
        scores = jnp.where(allowed[None], scores, masked_value)
        top = lax.optimization_barrier(jnp.max(scores, axis=-1, keepdims=True))
        weights = jnp.exp(scores - top)
        probs = low(weights / lax.optimization_barrier(jnp.sum(weights, axis=-1, keepdims=True)))
        return jnp.einsum('hqk,khd->qhd', probs, values, precision=HIGH)
    mixed = lax.map(jax.checkpoint(attend), jnp.arange(length // block, dtype=jnp.int32))
    mixed = low(low_back(mixed.reshape(length, heads * width)))
    branch = low_back(mat(mixed, proj_weight.reshape(heads * width, model)) + proj_bias)
    resid = seq_tokens + branch
    second = low(layer_norm(resid, gain_two, shift_two))
    hidden = low_back(mat(second, up_weight) + up_bias.reshape(-1))
    active = low(gelu_tanh(hidden))
    return resid + mat(active, down_weight) + down_bias

def reference(tokens, segments, gain_one, shift_one, qkv_weight, qv_bias, proj_weight, proj_bias, gain_two, shift_two, up_weight, up_bias, down_weight, down_bias, cotangent):
    params = (gain_one.astype(jnp.float32), shift_one.astype(jnp.float32), qkv_weight.astype(jnp.float32), qv_bias.astype(jnp.float32), proj_weight.astype(jnp.float32), proj_bias.astype(jnp.float32), gain_two.astype(jnp.float32), shift_two.astype(jnp.float32), up_weight.astype(jnp.float32), up_bias.astype(jnp.float32), down_weight.astype(jnp.float32), down_bias.astype(jnp.float32))

    def per_sequence(totals, item):
        seq_tokens, seq_segments, seq_cotangent = item

        def whole(values, *weights):
            return layer(values, seq_segments, *weights)
        result, pull = jax.vjp(whole, seq_tokens.astype(jnp.float32), *params)
        grads = pull(seq_cotangent.astype(jnp.float32))
        updated = tuple((total + grad for total, grad in zip(totals, grads[1:])))
        return (updated, (result.astype(jnp.bfloat16), grads[0]))
    zeros = tuple((jnp.zeros_like(param) for param in params))
    totals, (layer_out, input_grad) = lax.scan(per_sequence, zeros, (tokens, segments, cotangent))
    return (layer_out, input_grad, totals[0], totals[1], totals[2], totals[3], totals[4], totals[5], totals[6], totals[7], totals[8], totals[9], totals[10], totals[11])
```

```python
import jax
import jax.numpy as jnp
from jax import lax
from jax.experimental import pallas as pl
from jax.experimental.pallas import tpu as pltpu
from jax.sharding import PartitionSpec as P

eps_norm = 1e-05
masked_value = -1e30
gelu_coeff = 0.7978845608028654
vmem_bytes = 40 * 1024 * 1024


def layer_norm(values, gain, shift):
    center = values - jnp.mean(values, axis=-1, keepdims=True)
    spread = jnp.mean(center * center, axis=-1, keepdims=True)
    return center * lax.rsqrt(spread + eps_norm) * gain + shift


def gelu_tanh(values):
    return (
        0.5 * values * (1.0 + jnp.tanh(gelu_coeff * (values + 0.044715 * values * values * values)))
    )


def inner(left, right):
    return lax.dot_general(
        left, right, (((0,), (0,)), ((), ())), preferred_element_type=jnp.float32
    )


def outer(left, right):
    return lax.dot_general(
        left, right, (((1,), (1,)), ((), ())), preferred_element_type=jnp.float32
    )


def allowed_here(step, mine, block, seg_q_ref, seg_k_ref):
    query_pos = mine * block + lax.broadcasted_iota(jnp.int32, (block, block), 0)
    key_pos = step * block + lax.broadcasted_iota(jnp.int32, (block, block), 1)
    return (key_pos <= query_pos) & (seg_q_ref[:, :1] == seg_k_ref[0])


def forward_kernel(mine_ref, query_ref, pair_ref, seg_q_ref, seg_k_ref, out_ref, lse_ref, top, total, accum):
    step = pl.program_id(1)
    mine = mine_ref[0]
    block = query_ref.shape[0]

    @pl.when(step == 0)
    def _():
        top[...] = jnp.full_like(top, masked_value)
        total[...] = jnp.zeros_like(total)
        accum[...] = jnp.zeros_like(accum)

    @pl.when(step <= mine)
    def _():
        pair = pair_ref[...]
        scores = outer(query_ref[...], pair)
        scores = jnp.where(
            allowed_here(step, mine, block, seg_q_ref, seg_k_ref), scores, masked_value
        )
        old_top = top[...]
        new_top = jnp.maximum(old_top, jnp.max(scores, axis=-1, keepdims=True))
        weights = jnp.exp(scores - new_top)
        rescale = jnp.exp(old_top - new_top)
        total[...] = total[...] * rescale + jnp.sum(weights, axis=-1, keepdims=True)
        accum[...] = accum[...] * rescale + jnp.dot(
            weights.astype(jnp.bfloat16), pair, preferred_element_type=jnp.float32
        )
        top[...] = new_top

    @pl.when(step == pl.num_programs(1) - 1)
    def _():
        out_ref[...] = accum[...] / total[...]
        lse_ref[...] = jnp.broadcast_to(top[...] + jnp.log(total[...]), lse_ref.shape)


def backward_kernel(
    mine_ref, query_ref, grad_ref, mixed_ref, lse_ref, pair_ref, seg_q_ref, seg_k_ref,
    query_grad_ref, pair_grad_ref, accum, delta,
):
    step = pl.program_id(1)
    mine = mine_ref[0]
    block = query_ref.shape[0]

    @pl.when(step == 0)
    def _():
        accum[...] = jnp.zeros_like(accum)
        delta[...] = jnp.sum(
            grad_ref[...].astype(jnp.float32) * mixed_ref[...], axis=-1, keepdims=True
        )

    @pl.when(step <= mine)
    def _():
        pair = pair_ref[...]
        scores = outer(query_ref[...], pair)
        probs = jnp.where(
            allowed_here(step, mine, block, seg_q_ref, seg_k_ref),
            jnp.exp(scores - lse_ref[:, :1]),
            0.0,
        )
        prob_grad = outer(grad_ref[...], pair)
        score_low = (probs * (prob_grad - delta[...])).astype(jnp.bfloat16)
        accum[...] += jnp.dot(score_low, pair, preferred_element_type=jnp.float32)
        pair_grad_ref[...] = (
            inner(score_low, query_ref[...]) + inner(probs.astype(jnp.bfloat16), grad_ref[...])
        ).astype(pair_grad_ref.dtype)

    @pl.when(step > mine)
    def _():
        pair_grad_ref[...] = jnp.zeros_like(pair_grad_ref)

    @pl.when(step == pl.num_programs(1) - 1)
    def _():
        query_grad_ref[...] = accum[...]


def attend(head_size, mine, query_pad, pairs, seg_q, seg_k):
    block = query_pad.shape[0]
    lanes = pairs.shape[1]
    steps = pairs.shape[0] // block
    pair_wide = 2 * head_size
    heads_dev = lanes // pair_wide
    by_head = pl.BlockSpec((block, pair_wide), lambda h, j, m: (0, h))
    return pl.pallas_call(
        forward_kernel,
        grid_spec=pltpu.PrefetchScalarGridSpec(
            num_scalar_prefetch=1,
            grid=(heads_dev, steps),
            in_specs=[
                by_head,
                pl.BlockSpec((block, pair_wide), lambda h, j, m: (jnp.minimum(j, m[0]), h)),
                pl.BlockSpec((block, 128), lambda h, j, m: (0, 0)),
                pl.BlockSpec((1, 1, block), lambda h, j, m: (jnp.minimum(j, m[0]), 0, 0)),
            ],
            out_specs=[by_head, by_head],
            scratch_shapes=[
                pltpu.VMEM((block, 1), jnp.float32),
                pltpu.VMEM((block, 1), jnp.float32),
                pltpu.VMEM((block, pair_wide), jnp.float32),
            ],
        ),
        out_shape=[jax.ShapeDtypeStruct((block, lanes), jnp.float32)] * 2,
        compiler_params=pltpu.CompilerParams(vmem_limit_bytes=vmem_bytes),
        cost_estimate=pl.CostEstimate(
            flops=4 * block * pairs.shape[0] * lanes,
            bytes_accessed=4 * pairs.size,
            transcendentals=block * pairs.shape[0] * heads_dev,
        ),
    )(mine, query_pad, pairs, seg_q, seg_k)


def attend_back(head_size, mine, query_pad, grad_pad, mixed_wide, lse_wide, pairs, seg_q, seg_k):
    block = query_pad.shape[0]
    lanes = pairs.shape[1]
    steps = pairs.shape[0] // block
    pair_wide = 2 * head_size
    heads_dev = lanes // pair_wide
    by_head = pl.BlockSpec((block, pair_wide), lambda h, j, m: (0, h))
    return pl.pallas_call(
        backward_kernel,
        grid_spec=pltpu.PrefetchScalarGridSpec(
            num_scalar_prefetch=1,
            grid=(heads_dev, steps),
            in_specs=[
                by_head,
                by_head,
                by_head,
                by_head,
                pl.BlockSpec((block, pair_wide), lambda h, j, m: (jnp.minimum(j, m[0]), h)),
                pl.BlockSpec((block, 128), lambda h, j, m: (0, 0)),
                pl.BlockSpec((1, 1, block), lambda h, j, m: (jnp.minimum(j, m[0]), 0, 0)),
            ],
            out_specs=[by_head, pl.BlockSpec((block, pair_wide), lambda h, j, m: (j, h))],
            scratch_shapes=[
                pltpu.VMEM((block, pair_wide), jnp.float32),
                pltpu.VMEM((block, 1), jnp.float32),
            ],
        ),
        out_shape=[
            jax.ShapeDtypeStruct((block, lanes), jnp.float32),
            jax.ShapeDtypeStruct(pairs.shape, jnp.bfloat16),
        ],
        compiler_params=pltpu.CompilerParams(vmem_limit_bytes=vmem_bytes),
        cost_estimate=pl.CostEstimate(
            flops=10 * block * pairs.shape[0] * lanes,
            bytes_accessed=6 * pairs.size,
            transcendentals=block * pairs.shape[0] * heads_dev,
        ),
    )(mine, query_pad, grad_pad, mixed_wide, lse_wide, pairs, seg_q, seg_k)


def columns_of(vector, rows):
    count = -(-vector.shape[-1] // rows)
    padded = jnp.pad(vector, [(0, 0)] * (vector.ndim - 1) + [(0, count * rows - vector.shape[-1])])
    return padded.reshape(vector.shape[:-1] + (count, rows))


def pad_lanes(array):
    extra = -array.shape[-1] % 128
    return jnp.pad(array, [(0, 0)] * (array.ndim - 1) + [(0, extra)])


def gather_owned(array):
    return lax.all_gather(array, ("shard", "ctx"), axis=0, tiled=True)


def scatter_owned(array):
    return lax.psum_scatter(array, ("shard", "ctx"), scatter_dimension=0, tiled=True)


def sum_tp(array):
    return lax.psum(array, "tp")


def shards(
    tokens,
    segments,
    gain_one,
    shift_one,
    qkv_weight,
    qv_bias,
    proj_weight,
    proj_bias,
    gain_two,
    shift_two,
    up_weight,
    up_bias,
    down_weight,
    down_bias,
    cotangent,
):
    seq_count, block, width = tokens.shape
    rows = seq_count * block
    own = qkv_weight.shape[0]
    owners = width // own
    heads_dev = qkv_weight.shape[1]
    head_size = qkv_weight.shape[2] // 3
    hidden = up_weight.shape[1]
    mixed_wide = heads_dev * head_size
    scale = head_size ** (-0.5)
    ctx_size = lax.axis_size("ctx")
    ctx_index = lax.axis_index("ctx")
    shard_index = lax.axis_index("shard")
    low = jnp.bfloat16

    small = jnp.concatenate(
        [
            jnp.stack([gain_one, shift_one, proj_bias, gain_two, shift_two, down_bias]),
            columns_of(jnp.concatenate([qv_bias.reshape(-1), up_bias.reshape(-1)]), own),
            columns_of(segments.reshape(-1).astype(low), own),
        ],
        axis=0,
    )
    packed = jnp.concatenate(
        [
            up_weight,
            down_weight.T,
            qkv_weight.reshape(own, -1),
            proj_weight.reshape(mixed_wide, own).T,
            pad_lanes(small.T),
        ],
        axis=1,
    )
    whole = gather_owned(packed)
    at = 0
    up_full = whole[:, at : at + hidden]
    at += hidden
    down_full = whole[:, at : at + hidden]
    at += hidden
    qkv_full = whole[:, at : at + 3 * mixed_wide]
    at += 3 * mixed_wide
    proj_full = whole[:, at : at + mixed_wide]
    at += mixed_wide
    vectors = whole[:, at:].astype(jnp.float32).T
    gain_first, shift_first, bias_proj, gain_second, shift_second, bias_down = (
        vectors[i] for i in range(6)
    )
    by_owner = vectors.reshape(-1, owners, own)
    bias_each = qv_bias.size + up_bias.size
    bias_rows = -(-bias_each // own)
    bias_flat = (
        by_owner[6 : 6 + bias_rows].transpose(1, 0, 2).reshape(owners, -1)[:, :bias_each]
    )
    bias_qv = (
        bias_flat[:, : qv_bias.size]
        .reshape(owners, heads_dev, -1)
        .transpose(1, 0, 2)
        .reshape(heads_dev, 2 * head_size)
    )
    bias_up = (
        bias_flat[:, qv_bias.size :]
        .reshape(owners, up_bias.shape[0], -1)
        .transpose(1, 0, 2)
        .reshape(-1)
    )
    seg_rows = -(-rows // own)
    seg_all = (
        by_owner[6 + bias_rows : 6 + bias_rows + seg_rows]
        .transpose(1, 0, 2)
        .reshape(owners, -1)[:, :rows]
        .astype(jnp.int32)
    )
    seg_k = lax.dynamic_slice_in_dim(seg_all, shard_index * ctx_size, ctx_size, 0).reshape(
        ctx_size, 1, block
    )
    seg_q = jnp.broadcast_to(segments.reshape(block, 1), (block, 128))
    mine = ctx_index.astype(jnp.int32).reshape(1)

    flat = tokens.reshape(rows, width).astype(jnp.float32)
    norm_first, pull_first = jax.vjp(layer_norm, flat, gain_first, shift_first)
    input_low = norm_first.astype(low)
    projected = jnp.dot(input_low, qkv_full, preferred_element_type=jnp.float32).reshape(
        rows, heads_dev, 3 * head_size
    )
    keys_bias = jnp.concatenate(
        [jnp.zeros((heads_dev, head_size), jnp.float32), bias_qv[:, head_size:]], axis=1
    )
    pair_own = (projected[:, :, head_size:] + keys_bias).astype(low)
    query = (projected[:, :, :head_size] + bias_qv[:, :head_size]).astype(low)
    zero_half = jnp.zeros((rows, heads_dev, head_size), low)
    query_pad = jnp.concatenate([query * low(scale), zero_half], axis=2).reshape(
        rows, 2 * mixed_wide
    )
    pairs = lax.all_gather(pair_own.reshape(rows, 2 * mixed_wide), "ctx", axis=0, tiled=True)
    mixed_pad, lse_wide = attend(head_size, mine, query_pad, pairs, seg_q, seg_k)
    mixed_low = (
        mixed_pad.reshape(rows, heads_dev, 2 * head_size)[:, :, head_size:]
        .reshape(rows, mixed_wide)
        .astype(low)
    )
    branch = sum_tp(outer(mixed_low, proj_full).astype(low)).astype(jnp.float32) + bias_proj
    resid = flat + branch
    norm_second, pull_second = jax.vjp(layer_norm, resid, gain_second, shift_second)
    second_low = norm_second.astype(low)
    pre_act = jnp.dot(second_low, up_full, preferred_element_type=jnp.float32) + bias_up
    active, pull_gelu = jax.vjp(gelu_tanh, pre_act)
    active_low = active.astype(low)
    grad_low = cotangent.reshape(rows, width)
    grad_out = grad_low.astype(jnp.float32)
    act_grad = jnp.dot(grad_low, down_full, preferred_element_type=jnp.float32)
    (pre_grad,) = pull_gelu(act_grad)
    pre_low = pre_grad.astype(low)
    norm_two_grad = sum_tp(outer(pre_low, up_full).astype(low)).astype(jnp.float32)
    layer_out = (
        resid + sum_tp(outer(active_low, down_full).astype(low)).astype(jnp.float32) + bias_down
    )
    resid_part, gain_two_grad, shift_two_grad = pull_second(norm_two_grad)
    resid_grad = grad_out + resid_part
    branch_low = resid_grad.astype(low)
    mixed_grad = (
        jnp.dot(branch_low, proj_full, preferred_element_type=jnp.float32)
        .astype(low)
        .reshape(rows, heads_dev, head_size)
    )
    grad_pad = jnp.concatenate([zero_half, mixed_grad], axis=2).reshape(rows, 2 * mixed_wide)

    up_bias_grad = jnp.sum(pre_low.astype(jnp.float32), axis=0).reshape(up_bias.shape[0], -1)
    up_bias_split = columns_of(
        up_bias_grad.reshape(up_bias.shape[0], owners, -1).transpose(1, 0, 2).reshape(owners, -1),
        own,
    )
    second_small = jnp.concatenate(
        [
            jnp.stack(
                [
                    jnp.sum(grad_out, axis=0),
                    jnp.sum(branch_low.astype(jnp.float32), axis=0),
                    gain_two_grad,
                    shift_two_grad,
                ]
            ),
            up_bias_split.transpose(1, 0, 2).reshape(-1, width),
        ],
        axis=0,
    )
    second_piece = scatter_owned(
        pad_lanes(
            jnp.concatenate(
                [
                    inner(second_low, pre_low).astype(low),
                    inner(grad_low, active_low).astype(low),
                    inner(branch_low, mixed_low).astype(low),
                    second_small.T.astype(low),
                ],
                axis=1,
            )
        )
    ).astype(jnp.float32)

    query_grad, pair_total = attend_back(
        head_size, mine, query_pad, grad_pad, mixed_pad, lse_wide, pairs, seg_q, seg_k
    )
    pair_grad = lax.psum_scatter(pair_total, "ctx", scatter_dimension=0, tiled=True)
    query_part = (query_grad.reshape(rows, heads_dev, 2 * head_size)[:, :, :head_size] * scale).astype(
        low
    )
    proj_low = jnp.concatenate(
        [query_part, pair_grad.reshape(rows, heads_dev, 2 * head_size)], axis=2
    ).reshape(rows, 3 * mixed_wide)
    summed_bias = jnp.sum(proj_low.astype(jnp.float32), axis=0).reshape(heads_dev, 3 * head_size)
    qv_bias_grad = jnp.concatenate(
        [summed_bias[:, :head_size], summed_bias[:, 2 * head_size :]], axis=1
    )
    norm_one_grad = sum_tp(outer(proj_low, qkv_full).astype(low)).astype(jnp.float32)
    input_part, gain_one_grad, shift_one_grad = pull_first(norm_one_grad)
    input_grad = resid_grad + input_part
    qv_split = columns_of(
        qv_bias_grad.reshape(heads_dev, owners, -1).transpose(1, 0, 2).reshape(owners, -1), own
    )
    first_small = jnp.concatenate(
        [jnp.stack([gain_one_grad, shift_one_grad]), qv_split.transpose(1, 0, 2).reshape(-1, width)],
        axis=0,
    )
    first_piece = scatter_owned(
        pad_lanes(
            jnp.concatenate(
                [inner(input_low, proj_low).astype(low), first_small.T.astype(low)], axis=1
            )
        )
    ).astype(jnp.float32)

    up_piece = second_piece[:, :hidden]
    down_piece = second_piece[:, hidden : 2 * hidden].T
    at = 2 * hidden
    proj_piece = second_piece[:, at : at + mixed_wide].T.reshape(heads_dev, head_size, own)
    at += mixed_wide
    second_vectors = second_piece[:, at:].T
    up_bias_piece = second_vectors[4 : 4 + up_bias_split.shape[1]].reshape(-1)[
        : up_bias.size
    ].reshape(up_bias.shape)
    qkv_piece = first_piece[:, : 3 * mixed_wide].reshape(own, heads_dev, 3 * head_size)
    first_vectors = first_piece[:, 3 * mixed_wide :].T
    qv_bias_piece = first_vectors[2 : 2 + qv_split.shape[1]].reshape(-1)[: qv_bias.size].reshape(
        qv_bias.shape
    )
    return (
        layer_out.astype(low).reshape(seq_count, block, width),
        input_grad.reshape(seq_count, block, width),
        first_vectors[0],
        first_vectors[1],
        qkv_piece,
        qv_bias_piece,
        proj_piece,
        second_vectors[1],
        second_vectors[2],
        second_vectors[3],
        up_piece,
        up_bias_piece,
        down_piece,
        second_vectors[0],
    )


def solution(mesh):
    placed = (
        P("shard", "ctx", None),
        P("shard", "ctx"),
        P(("shard", "ctx")),
        P(("shard", "ctx")),
        P(("shard", "ctx"), "tp", None),
        P("tp", ("shard", "ctx")),
        P("tp", None, ("shard", "ctx")),
        P(("shard", "ctx")),
        P(("shard", "ctx")),
        P(("shard", "ctx")),
        P(("shard", "ctx"), "tp"),
        P("tp", ("shard", "ctx")),
        P("tp", ("shard", "ctx")),
        P(("shard", "ctx")),
        P("shard", "ctx", None),
    )
    return jax.shard_map(
        shards,
        mesh=mesh,
        in_specs=placed,
        out_specs=(
            P("shard", "ctx", None),
            P("shard", "ctx", None),
            P(("shard", "ctx")),
            P(("shard", "ctx")),
            P(("shard", "ctx"), "tp", None),
            P("tp", ("shard", "ctx")),
            P("tp", None, ("shard", "ctx")),
            P(("shard", "ctx")),
            P(("shard", "ctx")),
            P(("shard", "ctx")),
            P(("shard", "ctx"), "tp"),
            P("tp", ("shard", "ctx")),
            P("tp", ("shard", "ctx")),
            P(("shard", "ctx")),
        ),
        check_vma=False,
    )
```

```python
import jax
import jax.numpy as jnp
from jax import lax
from jax.experimental import pallas as pl
from jax.experimental.pallas import tpu as pltpu
from jax.sharding import PartitionSpec as P

eps_norm = 1e-05
masked_value = -1e30
gelu_coeff = 0.7978845608028654
vmem_bytes = 40 * 1024 * 1024


def layer_norm(values, gain, shift):
    center = values - jnp.mean(values, axis=-1, keepdims=True)
    spread = jnp.mean(center * center, axis=-1, keepdims=True)
    return center * lax.rsqrt(spread + eps_norm) * gain + shift


def gelu_tanh(values):
    return (
        0.5 * values * (1.0 + jnp.tanh(gelu_coeff * (values + 0.044715 * values * values * values)))
    )


def inner(left, right):
    return lax.dot_general(
        left, right, (((0,), (0,)), ((), ())), preferred_element_type=jnp.float32
    )


def outer(left, right):
    return lax.dot_general(
        left, right, (((1,), (1,)), ((), ())), preferred_element_type=jnp.float32
    )


def allowed_here(step, mine, block, seg_q_ref, seg_k_ref):
    query_pos = mine * block + lax.broadcasted_iota(jnp.int32, (block, block), 0)
    key_pos = step * block + lax.broadcasted_iota(jnp.int32, (block, block), 1)
    return (key_pos <= query_pos) & (seg_q_ref[:, :1] == seg_k_ref[0])


def forward_kernel(mine_ref, query_ref, pair_ref, seg_q_ref, seg_k_ref, out_ref, lse_ref, top, total, accum):
    step = pl.program_id(1)
    mine = mine_ref[0]
    block = query_ref.shape[0]

    @pl.when(step == 0)
    def _():
        top[...] = jnp.full_like(top, masked_value)
        total[...] = jnp.zeros_like(total)
        accum[...] = jnp.zeros_like(accum)

    @pl.when(step <= mine)
    def _():
        pair = pair_ref[...]
        scores = outer(query_ref[...], pair)
        scores = jnp.where(
            allowed_here(step, mine, block, seg_q_ref, seg_k_ref), scores, masked_value
        )
        old_top = top[...]
        new_top = jnp.maximum(old_top, jnp.max(scores, axis=-1, keepdims=True))
        weights = jnp.exp(scores - new_top)
        rescale = jnp.exp(old_top - new_top)
        total[...] = total[...] * rescale + jnp.sum(weights, axis=-1, keepdims=True)
        accum[...] = accum[...] * rescale + jnp.dot(
            weights.astype(jnp.bfloat16), pair, preferred_element_type=jnp.float32
        )
        top[...] = new_top

    @pl.when(step == pl.num_programs(1) - 1)
    def _():
        out_ref[...] = accum[...] / total[...]
        lse_ref[...] = jnp.broadcast_to(top[...] + jnp.log(total[...]), lse_ref.shape)


def backward_kernel(
    mine_ref, query_ref, grad_ref, mixed_ref, lse_ref, pair_ref, seg_q_ref, seg_k_ref,
    query_grad_ref, pair_grad_ref, accum, delta,
):
    step = pl.program_id(1)
    mine = mine_ref[0]
    block = query_ref.shape[0]

    @pl.when(step == 0)
    def _():
        accum[...] = jnp.zeros_like(accum)
        delta[...] = jnp.sum(
            grad_ref[...].astype(jnp.float32) * mixed_ref[...], axis=-1, keepdims=True
        )

    @pl.when(step <= mine)
    def _():
        pair = pair_ref[...]
        scores = outer(query_ref[...], pair)
        probs = jnp.where(
            allowed_here(step, mine, block, seg_q_ref, seg_k_ref),
            jnp.exp(scores - lse_ref[:, :1]),
            0.0,
        )
        prob_grad = outer(grad_ref[...], pair)
        score_low = (probs * (prob_grad - delta[...])).astype(jnp.bfloat16)
        accum[...] += jnp.dot(score_low, pair, preferred_element_type=jnp.float32)
        pair_grad_ref[...] = (
            inner(score_low, query_ref[...]) + inner(probs.astype(jnp.bfloat16), grad_ref[...])
        ).astype(pair_grad_ref.dtype)

    @pl.when(step > mine)
    def _():
        pair_grad_ref[...] = jnp.zeros_like(pair_grad_ref)

    @pl.when(step == pl.num_programs(1) - 1)
    def _():
        query_grad_ref[...] = accum[...]


def attend(head_size, mine, query_pad, pairs, seg_q, seg_k):
    block = query_pad.shape[0]
    lanes = pairs.shape[1]
    steps = pairs.shape[0] // block
    pair_wide = 2 * head_size
    heads_dev = lanes // pair_wide
    by_head = pl.BlockSpec((block, pair_wide), lambda h, j, m: (0, h))
    return pl.pallas_call(
        forward_kernel,
        grid_spec=pltpu.PrefetchScalarGridSpec(
            num_scalar_prefetch=1,
            grid=(heads_dev, steps),
            in_specs=[
                by_head,
                pl.BlockSpec((block, pair_wide), lambda h, j, m: (jnp.minimum(j, m[0]), h)),
                pl.BlockSpec((block, 128), lambda h, j, m: (0, 0)),
                pl.BlockSpec((1, 1, block), lambda h, j, m: (jnp.minimum(j, m[0]), 0, 0)),
            ],
            out_specs=[by_head, by_head],
            scratch_shapes=[
                pltpu.VMEM((block, 1), jnp.float32),
                pltpu.VMEM((block, 1), jnp.float32),
                pltpu.VMEM((block, pair_wide), jnp.float32),
            ],
        ),
        out_shape=[jax.ShapeDtypeStruct((block, lanes), jnp.float32)] * 2,
        compiler_params=pltpu.CompilerParams(vmem_limit_bytes=vmem_bytes),
        cost_estimate=pl.CostEstimate(
            flops=4 * block * pairs.shape[0] * lanes,
            bytes_accessed=4 * pairs.size,
            transcendentals=block * pairs.shape[0] * heads_dev,
        ),
    )(mine, query_pad, pairs, seg_q, seg_k)


def attend_back(head_size, mine, query_pad, grad_pad, mixed_wide, lse_wide, pairs, seg_q, seg_k):
    block = query_pad.shape[0]
    lanes = pairs.shape[1]
    steps = pairs.shape[0] // block
    pair_wide = 2 * head_size
    heads_dev = lanes // pair_wide
    by_head = pl.BlockSpec((block, pair_wide), lambda h, j, m: (0, h))
    return pl.pallas_call(
        backward_kernel,
        grid_spec=pltpu.PrefetchScalarGridSpec(
            num_scalar_prefetch=1,
            grid=(heads_dev, steps),
            in_specs=[
                by_head,
                by_head,
                by_head,
                by_head,
                pl.BlockSpec((block, pair_wide), lambda h, j, m: (jnp.minimum(j, m[0]), h)),
                pl.BlockSpec((block, 128), lambda h, j, m: (0, 0)),
                pl.BlockSpec((1, 1, block), lambda h, j, m: (jnp.minimum(j, m[0]), 0, 0)),
            ],
            out_specs=[by_head, pl.BlockSpec((block, pair_wide), lambda h, j, m: (j, h))],
            scratch_shapes=[
                pltpu.VMEM((block, pair_wide), jnp.float32),
                pltpu.VMEM((block, 1), jnp.float32),
            ],
        ),
        out_shape=[
            jax.ShapeDtypeStruct((block, lanes), jnp.float32),
            jax.ShapeDtypeStruct(pairs.shape, jnp.bfloat16),
        ],
        compiler_params=pltpu.CompilerParams(vmem_limit_bytes=vmem_bytes),
        cost_estimate=pl.CostEstimate(
            flops=10 * block * pairs.shape[0] * lanes,
            bytes_accessed=6 * pairs.size,
            transcendentals=block * pairs.shape[0] * heads_dev,
        ),
    )(mine, query_pad, grad_pad, mixed_wide, lse_wide, pairs, seg_q, seg_k)


def columns_of(vector, rows):
    count = -(-vector.shape[-1] // rows)
    padded = jnp.pad(vector, [(0, 0)] * (vector.ndim - 1) + [(0, count * rows - vector.shape[-1])])
    return padded.reshape(vector.shape[:-1] + (count, rows))


def pad_lanes(array):
    extra = -array.shape[-1] % 128
    return jnp.pad(array, [(0, 0)] * (array.ndim - 1) + [(0, extra)])


def gather_owned(array):
    return lax.all_gather(array, ("shard", "ctx"), axis=0, tiled=True)


def greet(partners):
    barrier = pltpu.get_barrier_semaphore()
    for partner in partners:
        pl.semaphore_signal(
            barrier, inc=1, device_id=partner, device_id_type=pl.DeviceIdType.MESH
        )
    pl.semaphore_wait(barrier, len(partners))


def send(source, target, send_sem, recv_sem, partner):
    copy = pltpu.make_async_remote_copy(
        src_ref=source,
        dst_ref=target,
        send_sem=send_sem,
        recv_sem=recv_sem,
        device_id=partner,
        device_id_type=pl.DeviceIdType.MESH,
    )
    copy.start()
    return copy


def wide(array):
    return array.astype(jnp.float32)


def sum_kernel(cuts, x_ref, out_ref, near_in, part, far_in, full, near_full, send_sems, recv_sems):
    me = lax.axis_index("tp")
    side = lax.rem(me, 2)
    near = {"tp": me + 1 - 2 * side}
    far = {"tp": lax.rem(me + 2, 4)}
    greet((near, far))
    half = x_ref.shape[0] // 2
    size = half // cuts
    mine, other = side * half, (1 - side) * half
    copies = [[], [], []]

    def rows_at(base, k):
        return pl.ds(pl.multiple_of(base + k * size, size), size)

    for k in range(cuts):
        here = pl.ds(k * size, size)
        copies[0].append(
            send(
                x_ref.at[rows_at(other, k)], near_in.at[here],
                send_sems.at[0, k], recv_sems.at[0, k], near,
            )
        )
    for k in range(cuts):
        here = pl.ds(k * size, size)
        copies[0][k].wait_recv()
        part[here] = (wide(x_ref[rows_at(mine, k)]) + wide(near_in[here])).astype(part.dtype)
        copies[1].append(
            send(part.at[here], far_in.at[here], send_sems.at[1, k], recv_sems.at[1, k], far)
        )
    for k in range(cuts):
        here = pl.ds(k * size, size)
        copies[1][k].wait_recv()
        total = (wide(part[here]) + wide(far_in[here])).astype(full.dtype)
        full[here] = total
        copies[2].append(
            send(full.at[here], near_full.at[here], send_sems.at[2, k], recv_sems.at[2, k], near)
        )
        out_ref[rows_at(mine, k)] = total
    for k in range(cuts):
        copies[2][k].wait_recv()
        out_ref[rows_at(other, k)] = near_full[pl.ds(k * size, size)]
    for group in copies:
        for copy in group:
            copy.wait_send()


def sum_tp_direct(array):
    rows, width = array.shape
    if lax.axis_size("tp") != 4 or rows % 128 != 0:
        return lax.psum(array, "tp")
    cuts = 4
    vmem = pl.BlockSpec(memory_space=pltpu.VMEM)

    def kernel(*refs):
        sum_kernel(cuts, *refs)

    return pl.pallas_call(
        kernel,
        out_shape=jax.ShapeDtypeStruct(array.shape, array.dtype),
        in_specs=[vmem],
        out_specs=vmem,
        scratch_shapes=[pltpu.VMEM((rows // 2, width), array.dtype)] * 5
        + [pltpu.SemaphoreType.DMA((3, cuts)), pltpu.SemaphoreType.DMA((3, cuts))],
        compiler_params=pltpu.CompilerParams(
            collective_id=0, has_side_effects=True, vmem_limit_bytes=vmem_bytes
        ),
    )(array)


def scatter_kernel(
    bounds, count, x_ref, out_ref, shard_in, part, ctx_in, shard_send, shard_recv, ctx_send, ctx_recv
):
    mine = lax.axis_index("shard")
    place = lax.axis_index("ctx")
    across = {"shard": 1 - mine}
    targets = [lax.rem(place + hop, count) for hop in range(1, count)]
    greet([across] + [{"ctx": target} for target in targets])
    first = []
    second = []
    for k, (low_at, size) in enumerate(bounds):
        lanes = pl.ds(low_at, size)
        first.append(
            send(
                x_ref.at[pl.ds((1 - mine) * count, count), :, lanes], shard_in.at[:, :, lanes],
                shard_send.at[k], shard_recv.at[k], across,
            )
        )
    for k, (low_at, size) in enumerate(bounds):
        lanes = pl.ds(low_at, size)
        first[k].wait_recv()
        part[:, :, lanes] = (
            wide(x_ref[pl.ds(mine * count, count), :, lanes]) + wide(shard_in[:, :, lanes])
        ).astype(part.dtype)
        second.append(
            [
                send(
                    part.at[target, :, lanes], ctx_in.at[hop, :, lanes],
                    ctx_send.at[hop, k], ctx_recv.at[hop, k], {"ctx": target},
                )
                for hop, target in enumerate(targets)
            ]
        )
    for k, (low_at, size) in enumerate(bounds):
        lanes = pl.ds(low_at, size)
        total = wide(part[place, :, lanes])
        for hop in range(count - 1):
            second[k][hop].wait_recv()
            total = total + wide(ctx_in[hop, :, lanes])
        out_ref[:, lanes] = total
    for k in range(len(bounds)):
        first[k].wait_send()
        for copy in second[k]:
            copy.wait_send()


def scatter_owned(array):
    shard_size, count = lax.axis_size("shard"), lax.axis_size("ctx")
    own, lanes = array.shape[0] // (shard_size * count), array.shape[1]
    if shard_size != 2:
        return lax.psum_scatter(
            array, ("shard", "ctx"), scatter_dimension=0, tiled=True
        ).astype(jnp.float32)
    step = 512
    bounds = [(at, min(step, lanes - at)) for at in range(0, lanes, step)]
    vmem = pl.BlockSpec(memory_space=pltpu.VMEM)

    def kernel(*refs):
        scatter_kernel(bounds, count, *refs)

    parts = len(bounds)
    return pl.pallas_call(
        kernel,
        out_shape=jax.ShapeDtypeStruct((own, lanes), jnp.float32),
        in_specs=[vmem],
        out_specs=vmem,
        scratch_shapes=[
            pltpu.VMEM((count, own, lanes), array.dtype),
            pltpu.VMEM((count, own, lanes), array.dtype),
            pltpu.VMEM((count - 1, own, lanes), array.dtype),
            pltpu.SemaphoreType.DMA((parts,)),
            pltpu.SemaphoreType.DMA((parts,)),
            pltpu.SemaphoreType.DMA((count - 1, parts)),
            pltpu.SemaphoreType.DMA((count - 1, parts)),
        ],
        compiler_params=pltpu.CompilerParams(
            collective_id=1, has_side_effects=True, vmem_limit_bytes=vmem_bytes
        ),
    )(array.reshape(shard_size * count, own, lanes))


def sum_tp(array):
    return lax.psum(array, "tp")


def shards(
    tokens,
    segments,
    gain_one,
    shift_one,
    qkv_weight,
    qv_bias,
    proj_weight,
    proj_bias,
    gain_two,
    shift_two,
    up_weight,
    up_bias,
    down_weight,
    down_bias,
    cotangent,
):
    seq_count, block, width = tokens.shape
    rows = seq_count * block
    own = qkv_weight.shape[0]
    owners = width // own
    heads_dev = qkv_weight.shape[1]
    head_size = qkv_weight.shape[2] // 3
    hidden = up_weight.shape[1]
    mixed_wide = heads_dev * head_size
    scale = head_size ** (-0.5)
    ctx_size = lax.axis_size("ctx")
    ctx_index = lax.axis_index("ctx")
    shard_index = lax.axis_index("shard")
    low = jnp.bfloat16

    small = jnp.concatenate(
        [
            jnp.stack([gain_one, shift_one, proj_bias, gain_two, shift_two, down_bias]),
            columns_of(jnp.concatenate([qv_bias.reshape(-1), up_bias.reshape(-1)]), own),
            columns_of(segments.reshape(-1).astype(low), own),
        ],
        axis=0,
    )
    packed = jnp.concatenate(
        [
            up_weight,
            down_weight.T,
            qkv_weight.reshape(own, -1),
            proj_weight.reshape(mixed_wide, own).T,
            pad_lanes(small.T),
        ],
        axis=1,
    )
    whole = gather_owned(packed)
    at = 0
    up_full = whole[:, at : at + hidden]
    at += hidden
    down_full = whole[:, at : at + hidden]
    at += hidden
    qkv_full = whole[:, at : at + 3 * mixed_wide]
    at += 3 * mixed_wide
    proj_full = whole[:, at : at + mixed_wide]
    at += mixed_wide
    vectors = whole[:, at:].astype(jnp.float32).T
    gain_first, shift_first, bias_proj, gain_second, shift_second, bias_down = (
        vectors[i] for i in range(6)
    )
    by_owner = vectors.reshape(-1, owners, own)
    bias_each = qv_bias.size + up_bias.size
    bias_rows = -(-bias_each // own)
    bias_flat = (
        by_owner[6 : 6 + bias_rows].transpose(1, 0, 2).reshape(owners, -1)[:, :bias_each]
    )
    bias_qv = (
        bias_flat[:, : qv_bias.size]
        .reshape(owners, heads_dev, -1)
        .transpose(1, 0, 2)
        .reshape(heads_dev, 2 * head_size)
    )
    bias_up = (
        bias_flat[:, qv_bias.size :]
        .reshape(owners, up_bias.shape[0], -1)
        .transpose(1, 0, 2)
        .reshape(-1)
    )
    seg_rows = -(-rows // own)
    seg_all = (
        by_owner[6 + bias_rows : 6 + bias_rows + seg_rows]
        .transpose(1, 0, 2)
        .reshape(owners, -1)[:, :rows]
        .astype(jnp.int32)
    )
    seg_k = lax.dynamic_slice_in_dim(seg_all, shard_index * ctx_size, ctx_size, 0).reshape(
        ctx_size, 1, block
    )
    seg_q = jnp.broadcast_to(segments.reshape(block, 1), (block, 128))
    mine = ctx_index.astype(jnp.int32).reshape(1)

    flat = tokens.reshape(rows, width).astype(jnp.float32)
    norm_first, pull_first = jax.vjp(layer_norm, flat, gain_first, shift_first)
    input_low = norm_first.astype(low)
    projected = jnp.dot(input_low, qkv_full, preferred_element_type=jnp.float32).reshape(
        rows, heads_dev, 3 * head_size
    )
    keys_bias = jnp.concatenate(
        [jnp.zeros((heads_dev, head_size), jnp.float32), bias_qv[:, head_size:]], axis=1
    )
    pair_own = (projected[:, :, head_size:] + keys_bias).astype(low)
    query = (projected[:, :, :head_size] + bias_qv[:, :head_size]).astype(low)
    zero_half = jnp.zeros((rows, heads_dev, head_size), low)
    query_pad = jnp.concatenate([query * low(scale), zero_half], axis=2).reshape(
        rows, 2 * mixed_wide
    )
    pairs = lax.all_gather(pair_own.reshape(rows, 2 * mixed_wide), "ctx", axis=0, tiled=True)
    mixed_pad, lse_wide = attend(head_size, mine, query_pad, pairs, seg_q, seg_k)
    mixed_low = (
        mixed_pad.reshape(rows, heads_dev, 2 * head_size)[:, :, head_size:]
        .reshape(rows, mixed_wide)
        .astype(low)
    )
    branch = sum_tp_direct(outer(mixed_low, proj_full).astype(low)).astype(jnp.float32) + bias_proj
    resid = flat + branch
    norm_second, pull_second = jax.vjp(layer_norm, resid, gain_second, shift_second)
    second_low = norm_second.astype(low)
    pre_act = jnp.dot(second_low, up_full, preferred_element_type=jnp.float32) + bias_up
    active, pull_gelu = jax.vjp(gelu_tanh, pre_act)
    active_low = active.astype(low)
    grad_low = cotangent.reshape(rows, width)
    grad_out = grad_low.astype(jnp.float32)
    act_grad = jnp.dot(grad_low, down_full, preferred_element_type=jnp.float32)
    (pre_grad,) = pull_gelu(act_grad)
    pre_low = pre_grad.astype(low)
    norm_two_grad = sum_tp_direct(outer(pre_low, up_full).astype(low)).astype(jnp.float32)
    layer_out = (
        resid + sum_tp(outer(active_low, down_full).astype(low)).astype(jnp.float32) + bias_down
    )
    resid_part, gain_two_grad, shift_two_grad = pull_second(norm_two_grad)
    resid_grad = grad_out + resid_part
    branch_low = resid_grad.astype(low)
    mixed_grad = (
        jnp.dot(branch_low, proj_full, preferred_element_type=jnp.float32)
        .astype(low)
        .reshape(rows, heads_dev, head_size)
    )
    grad_pad = jnp.concatenate([zero_half, mixed_grad], axis=2).reshape(rows, 2 * mixed_wide)

    up_bias_grad = jnp.sum(pre_low.astype(jnp.float32), axis=0).reshape(up_bias.shape[0], -1)
    up_bias_split = columns_of(
        up_bias_grad.reshape(up_bias.shape[0], owners, -1).transpose(1, 0, 2).reshape(owners, -1),
        own,
    )
    second_small = jnp.concatenate(
        [
            jnp.stack(
                [
                    jnp.sum(grad_out, axis=0),
                    jnp.sum(branch_low.astype(jnp.float32), axis=0),
                    gain_two_grad,
                    shift_two_grad,
                ]
            ),
            up_bias_split.transpose(1, 0, 2).reshape(-1, width),
        ],
        axis=0,
    )
    query_grad, pair_total = attend_back(
        head_size, mine, query_pad, grad_pad, mixed_pad, lse_wide, pairs, seg_q, seg_k
    )
    pair_grad = lax.psum_scatter(pair_total, "ctx", scatter_dimension=0, tiled=True)
    query_part = (query_grad.reshape(rows, heads_dev, 2 * head_size)[:, :, :head_size] * scale).astype(
        low
    )
    proj_low = jnp.concatenate(
        [query_part, pair_grad.reshape(rows, heads_dev, 2 * head_size)], axis=2
    ).reshape(rows, 3 * mixed_wide)
    summed_bias = jnp.sum(proj_low.astype(jnp.float32), axis=0).reshape(heads_dev, 3 * head_size)
    qv_bias_grad = jnp.concatenate(
        [summed_bias[:, :head_size], summed_bias[:, 2 * head_size :]], axis=1
    )
    norm_one_grad = sum_tp_direct(outer(proj_low, qkv_full).astype(low)).astype(jnp.float32)
    input_part, gain_one_grad, shift_one_grad = pull_first(norm_one_grad)
    input_grad = resid_grad + input_part
    qv_split = columns_of(
        qv_bias_grad.reshape(heads_dev, owners, -1).transpose(1, 0, 2).reshape(owners, -1), own
    )
    first_small = jnp.concatenate(
        [jnp.stack([gain_one_grad, shift_one_grad]), qv_split.transpose(1, 0, 2).reshape(-1, width)],
        axis=0,
    )
    small_count = second_small.shape[0]
    pieces = scatter_owned(
        jnp.concatenate(
            [
                inner(second_low, pre_low).astype(low),
                inner(grad_low, active_low).astype(low),
                inner(input_low, proj_low).astype(low),
                inner(branch_low, mixed_low).astype(low),
                pad_lanes(jnp.concatenate([second_small, first_small], axis=0).T.astype(low)),
            ],
            axis=1,
        )
    )
    up_piece = pieces[:, :hidden]
    down_piece = pieces[:, hidden : 2 * hidden].T
    at = 2 * hidden
    qkv_piece = pieces[:, at : at + 3 * mixed_wide].reshape(own, heads_dev, 3 * head_size)
    at += 3 * mixed_wide
    proj_piece = pieces[:, at : at + mixed_wide].T.reshape(heads_dev, head_size, own)
    at += mixed_wide
    second_vectors = pieces[:, at : at + small_count].T
    first_vectors = pieces[:, at + small_count : at + small_count + first_small.shape[0]].T
    up_bias_piece = second_vectors[4:].reshape(-1)[: up_bias.size].reshape(up_bias.shape)
    qv_bias_piece = first_vectors[2:].reshape(-1)[: qv_bias.size].reshape(qv_bias.shape)
    return (
        layer_out.astype(low).reshape(seq_count, block, width),
        input_grad.reshape(seq_count, block, width),
        first_vectors[0],
        first_vectors[1],
        qkv_piece,
        qv_bias_piece,
        proj_piece,
        second_vectors[1],
        second_vectors[2],
        second_vectors[3],
        up_piece,
        up_bias_piece,
        down_piece,
        second_vectors[0],
    )


def solution(mesh):
    placed = (
        P("shard", "ctx", None),
        P("shard", "ctx"),
        P(("shard", "ctx")),
        P(("shard", "ctx")),
        P(("shard", "ctx"), "tp", None),
        P("tp", ("shard", "ctx")),
        P("tp", None, ("shard", "ctx")),
        P(("shard", "ctx")),
        P(("shard", "ctx")),
        P(("shard", "ctx")),
        P(("shard", "ctx"), "tp"),
        P("tp", ("shard", "ctx")),
        P("tp", ("shard", "ctx")),
        P(("shard", "ctx")),
        P("shard", "ctx", None),
    )
    return jax.shard_map(
        shards,
        mesh=mesh,
        in_specs=placed,
        out_specs=(
            P("shard", "ctx", None),
            P("shard", "ctx", None),
            P(("shard", "ctx")),
            P(("shard", "ctx")),
            P(("shard", "ctx"), "tp", None),
            P("tp", ("shard", "ctx")),
            P("tp", None, ("shard", "ctx")),
            P(("shard", "ctx")),
            P(("shard", "ctx")),
            P(("shard", "ctx")),
            P(("shard", "ctx"), "tp"),
            P("tp", ("shard", "ctx")),
            P("tp", ("shard", "ctx")),
            P(("shard", "ctx")),
        ),
        check_vma=False,
    )
```

```python
import jax
import jax.numpy as jnp
from jax import lax
from jax.experimental import pallas as pl
from jax.experimental.pallas import tpu as pltpu
from jax.sharding import PartitionSpec as P

eps_norm = 1e-05
masked_value = -1e30
gelu_coeff = 0.7978845608028654
vmem_bytes = 40 * 1024 * 1024


def layer_norm(values, gain, shift):
    center = values - jnp.mean(values, axis=-1, keepdims=True)
    spread = jnp.mean(center * center, axis=-1, keepdims=True)
    return center * lax.rsqrt(spread + eps_norm) * gain + shift


def gelu_tanh(values):
    return (
        0.5 * values * (1.0 + jnp.tanh(gelu_coeff * (values + 0.044715 * values * values * values)))
    )


def inner(left, right):
    return lax.dot_general(
        left, right, (((0,), (0,)), ((), ())), preferred_element_type=jnp.float32
    )


def outer(left, right):
    return lax.dot_general(
        left, right, (((1,), (1,)), ((), ())), preferred_element_type=jnp.float32
    )


def allowed_here(step, mine, block, seg_q_ref, seg_k_ref):
    query_pos = mine * block + lax.broadcasted_iota(jnp.int32, (block, block), 0)
    key_pos = step * block + lax.broadcasted_iota(jnp.int32, (block, block), 1)
    return (key_pos <= query_pos) & (seg_q_ref[:, :1] == seg_k_ref[0])


def forward_kernel(mine_ref, query_ref, pair_ref, seg_q_ref, seg_k_ref, out_ref, lse_ref, top, total, accum):
    step = pl.program_id(1)
    mine = mine_ref[0]
    block = query_ref.shape[0]

    @pl.when(step == 0)
    def _():
        top[...] = jnp.full_like(top, masked_value)
        total[...] = jnp.zeros_like(total)
        accum[...] = jnp.zeros_like(accum)

    @pl.when(step <= mine)
    def _():
        pair = pair_ref[...]
        scores = outer(query_ref[...], pair)
        scores = jnp.where(
            allowed_here(step, mine, block, seg_q_ref, seg_k_ref), scores, masked_value
        )
        old_top = top[...]
        new_top = jnp.maximum(old_top, jnp.max(scores, axis=-1, keepdims=True))
        weights = jnp.exp(scores - new_top)
        rescale = jnp.exp(old_top - new_top)
        total[...] = total[...] * rescale + jnp.sum(weights, axis=-1, keepdims=True)
        accum[...] = accum[...] * rescale + jnp.dot(
            weights.astype(jnp.bfloat16), pair, preferred_element_type=jnp.float32
        )
        top[...] = new_top

    @pl.when(step == pl.num_programs(1) - 1)
    def _():
        out_ref[...] = accum[...] / total[...]
        lse_ref[...] = jnp.broadcast_to(top[...] + jnp.log(total[...]), lse_ref.shape)


def backward_kernel(
    mine_ref, query_ref, grad_ref, mixed_ref, lse_ref, pair_ref, seg_q_ref, seg_k_ref,
    query_grad_ref, pair_grad_ref, accum, delta,
):
    step = pl.program_id(1)
    mine = mine_ref[0]
    block = query_ref.shape[0]

    @pl.when(step == 0)
    def _():
        accum[...] = jnp.zeros_like(accum)
        delta[...] = jnp.sum(
            grad_ref[...].astype(jnp.float32) * mixed_ref[...], axis=-1, keepdims=True
        )

    @pl.when(step <= mine)
    def _():
        pair = pair_ref[...]
        scores = outer(query_ref[...], pair)
        probs = jnp.where(
            allowed_here(step, mine, block, seg_q_ref, seg_k_ref),
            jnp.exp(scores - lse_ref[:, :1]),
            0.0,
        )
        prob_grad = outer(grad_ref[...], pair)
        score_low = (probs * (prob_grad - delta[...])).astype(jnp.bfloat16)
        accum[...] += jnp.dot(score_low, pair, preferred_element_type=jnp.float32)
        pair_grad_ref[...] = (
            inner(score_low, query_ref[...]) + inner(probs.astype(jnp.bfloat16), grad_ref[...])
        ).astype(pair_grad_ref.dtype)

    @pl.when(step > mine)
    def _():
        pair_grad_ref[...] = jnp.zeros_like(pair_grad_ref)

    @pl.when(step == pl.num_programs(1) - 1)
    def _():
        query_grad_ref[...] = accum[...]


def attend(head_size, mine, query_pad, pairs, seg_q, seg_k):
    block = query_pad.shape[0]
    lanes = pairs.shape[1]
    steps = pairs.shape[0] // block
    pair_wide = 2 * head_size
    heads_dev = lanes // pair_wide
    by_head = pl.BlockSpec((block, pair_wide), lambda h, j, m: (0, h))
    return pl.pallas_call(
        forward_kernel,
        grid_spec=pltpu.PrefetchScalarGridSpec(
            num_scalar_prefetch=1,
            grid=(heads_dev, steps),
            in_specs=[
                by_head,
                pl.BlockSpec((block, pair_wide), lambda h, j, m: (jnp.minimum(j, m[0]), h)),
                pl.BlockSpec((block, 128), lambda h, j, m: (0, 0)),
                pl.BlockSpec((1, 1, block), lambda h, j, m: (jnp.minimum(j, m[0]), 0, 0)),
            ],
            out_specs=[by_head, by_head],
            scratch_shapes=[
                pltpu.VMEM((block, 1), jnp.float32),
                pltpu.VMEM((block, 1), jnp.float32),
                pltpu.VMEM((block, pair_wide), jnp.float32),
            ],
        ),
        out_shape=[jax.ShapeDtypeStruct((block, lanes), jnp.float32)] * 2,
        compiler_params=pltpu.CompilerParams(vmem_limit_bytes=vmem_bytes),
        cost_estimate=pl.CostEstimate(
            flops=4 * block * pairs.shape[0] * lanes,
            bytes_accessed=4 * pairs.size,
            transcendentals=block * pairs.shape[0] * heads_dev,
        ),
    )(mine, query_pad, pairs, seg_q, seg_k)


def attend_back(head_size, mine, query_pad, grad_pad, mixed_wide, lse_wide, pairs, seg_q, seg_k):
    block = query_pad.shape[0]
    lanes = pairs.shape[1]
    steps = pairs.shape[0] // block
    pair_wide = 2 * head_size
    heads_dev = lanes // pair_wide
    by_head = pl.BlockSpec((block, pair_wide), lambda h, j, m: (0, h))
    return pl.pallas_call(
        backward_kernel,
        grid_spec=pltpu.PrefetchScalarGridSpec(
            num_scalar_prefetch=1,
            grid=(heads_dev, steps),
            in_specs=[
                by_head,
                by_head,
                by_head,
                by_head,
                pl.BlockSpec((block, pair_wide), lambda h, j, m: (jnp.minimum(j, m[0]), h)),
                pl.BlockSpec((block, 128), lambda h, j, m: (0, 0)),
                pl.BlockSpec((1, 1, block), lambda h, j, m: (jnp.minimum(j, m[0]), 0, 0)),
            ],
            out_specs=[by_head, pl.BlockSpec((block, pair_wide), lambda h, j, m: (j, h))],
            scratch_shapes=[
                pltpu.VMEM((block, pair_wide), jnp.float32),
                pltpu.VMEM((block, 1), jnp.float32),
            ],
        ),
        out_shape=[
            jax.ShapeDtypeStruct((block, lanes), jnp.float32),
            jax.ShapeDtypeStruct(pairs.shape, jnp.bfloat16),
        ],
        compiler_params=pltpu.CompilerParams(vmem_limit_bytes=vmem_bytes),
        cost_estimate=pl.CostEstimate(
            flops=10 * block * pairs.shape[0] * lanes,
            bytes_accessed=6 * pairs.size,
            transcendentals=block * pairs.shape[0] * heads_dev,
        ),
    )(mine, query_pad, grad_pad, mixed_wide, lse_wide, pairs, seg_q, seg_k)


def columns_of(vector, rows):
    count = -(-vector.shape[-1] // rows)
    padded = jnp.pad(vector, [(0, 0)] * (vector.ndim - 1) + [(0, count * rows - vector.shape[-1])])
    return padded.reshape(vector.shape[:-1] + (count, rows))


def pad_lanes(array):
    extra = -array.shape[-1] % 128
    return jnp.pad(array, [(0, 0)] * (array.ndim - 1) + [(0, extra)])


def greet(partners):
    barrier = pltpu.get_barrier_semaphore()
    for partner in partners:
        pl.semaphore_signal(
            barrier, inc=1, device_id=partner, device_id_type=pl.DeviceIdType.MESH
        )
    pl.semaphore_wait(barrier, len(partners))


def send(source, target, send_sem, recv_sem, partner):
    copy = pltpu.make_async_remote_copy(
        src_ref=source,
        dst_ref=target,
        send_sem=send_sem,
        recv_sem=recv_sem,
        device_id=partner,
        device_id_type=pl.DeviceIdType.MESH,
    )
    copy.start()
    return copy


def wide(array):
    return array.astype(jnp.float32)


def gather_kernel(
    bounds, count, x_ref, out_ref, shard_send, shard_recv, ctx_send, ctx_recv
):
    mine = lax.axis_index("shard")
    place = lax.axis_index("ctx")
    across = {"shard": 1 - mine}
    targets = [lax.rem(place + hop, count) for hop in range(1, count)]
    greet([across] + [{"ctx": target} for target in targets])
    here = mine * count + place
    first = []
    second = []
    for k, (low_at, size) in enumerate(bounds):
        lanes = pl.ds(low_at, size)
        first.append(
            [
                send(
                    x_ref.at[:, lanes], out_ref.at[here, :, lanes],
                    ctx_send.at[hop, k], ctx_recv.at[hop, k], {"ctx": target},
                )
                for hop, target in enumerate(targets)
            ]
        )
        second.append(
            [
                send(
                    x_ref.at[:, lanes], out_ref.at[here, :, lanes],
                    shard_send.at[0, k], shard_recv.at[0, k], across,
                )
            ]
        )
    out_ref[here] = x_ref[...]
    for k, (low_at, size) in enumerate(bounds):
        lanes = pl.ds(low_at, size)
        for hop in range(1, count):
            arrived = mine * count + lax.rem(place - hop + count, count)
            first[k][hop - 1].wait_recv()
            second[k].append(
                send(
                    out_ref.at[arrived, :, lanes], out_ref.at[arrived, :, lanes],
                    shard_send.at[hop, k], shard_recv.at[hop, k], across,
                )
            )
    for k in range(len(bounds)):
        for copy in second[k]:
            copy.wait()
        for copy in first[k]:
            copy.wait_send()


def gather_owned(array):
    shard_size, count = lax.axis_size("shard"), lax.axis_size("ctx")
    own, lanes = array.shape
    if shard_size != 2:
        return lax.all_gather(array, ("shard", "ctx"), axis=0, tiled=True)
    step = 896
    bounds = [(at, min(step, lanes - at)) for at in range(0, lanes, step)]
    vmem = pl.BlockSpec(memory_space=pltpu.VMEM)

    def kernel(*refs):
        gather_kernel(bounds, count, *refs)

    parts = len(bounds)
    return pl.pallas_call(
        kernel,
        out_shape=jax.ShapeDtypeStruct((shard_size * count, own, lanes), array.dtype),
        in_specs=[vmem],
        out_specs=vmem,
        scratch_shapes=[
            pltpu.SemaphoreType.DMA((count, parts)),
            pltpu.SemaphoreType.DMA((count, parts)),
            pltpu.SemaphoreType.DMA((count - 1, parts)),
            pltpu.SemaphoreType.DMA((count - 1, parts)),
        ],
        compiler_params=pltpu.CompilerParams(
            collective_id=2, has_side_effects=True, vmem_limit_bytes=vmem_bytes
        ),
    )(array).reshape(shard_size * count * own, lanes)


def sum_kernel(cuts, x_ref, out_ref, near_in, part, far_in, full, near_full, send_sems, recv_sems):
    me = lax.axis_index("tp")
    side = lax.rem(me, 2)
    near = {"tp": me + 1 - 2 * side}
    far = {"tp": lax.rem(me + 2, 4)}
    greet((near, far))
    half = x_ref.shape[0] // 2
    size = half // cuts
    mine, other = side * half, (1 - side) * half
    copies = [[], [], []]

    def rows_at(base, k):
        return pl.ds(pl.multiple_of(base + k * size, size), size)

    for k in range(cuts):
        here = pl.ds(k * size, size)
        copies[0].append(
            send(
                x_ref.at[rows_at(other, k)], near_in.at[here],
                send_sems.at[0, k], recv_sems.at[0, k], near,
            )
        )
    for k in range(cuts):
        here = pl.ds(k * size, size)
        copies[0][k].wait_recv()
        part[here] = (wide(x_ref[rows_at(mine, k)]) + wide(near_in[here])).astype(part.dtype)
        copies[1].append(
            send(part.at[here], far_in.at[here], send_sems.at[1, k], recv_sems.at[1, k], far)
        )
    for k in range(cuts):
        here = pl.ds(k * size, size)
        copies[1][k].wait_recv()
        total = (wide(part[here]) + wide(far_in[here])).astype(full.dtype)
        full[here] = total
        copies[2].append(
            send(full.at[here], near_full.at[here], send_sems.at[2, k], recv_sems.at[2, k], near)
        )
        out_ref[rows_at(mine, k)] = total
    for k in range(cuts):
        copies[2][k].wait_recv()
        out_ref[rows_at(other, k)] = near_full[pl.ds(k * size, size)]
    for group in copies:
        for copy in group:
            copy.wait_send()


def sum_tp_direct(array):
    rows, width = array.shape
    if lax.axis_size("tp") != 4 or rows % 128 != 0:
        return lax.psum(array, "tp")
    cuts = 4
    vmem = pl.BlockSpec(memory_space=pltpu.VMEM)

    def kernel(*refs):
        sum_kernel(cuts, *refs)

    return pl.pallas_call(
        kernel,
        out_shape=jax.ShapeDtypeStruct(array.shape, array.dtype),
        in_specs=[vmem],
        out_specs=vmem,
        scratch_shapes=[pltpu.VMEM((rows // 2, width), array.dtype)] * 5
        + [pltpu.SemaphoreType.DMA((3, cuts)), pltpu.SemaphoreType.DMA((3, cuts))],
        compiler_params=pltpu.CompilerParams(
            collective_id=0, has_side_effects=True, vmem_limit_bytes=vmem_bytes
        ),
    )(array)


def scatter_kernel(
    bounds, count, x_ref, out_ref, shard_in, part, ctx_in, shard_send, shard_recv, ctx_send, ctx_recv
):
    mine = lax.axis_index("shard")
    place = lax.axis_index("ctx")
    across = {"shard": 1 - mine}
    targets = [lax.rem(place + hop, count) for hop in range(1, count)]
    greet([across] + [{"ctx": target} for target in targets])
    first = []
    second = []
    for k, (low_at, size) in enumerate(bounds):
        lanes = pl.ds(low_at, size)
        first.append(
            send(
                x_ref.at[pl.ds((1 - mine) * count, count), :, lanes], shard_in.at[:, :, lanes],
                shard_send.at[k], shard_recv.at[k], across,
            )
        )
    for k, (low_at, size) in enumerate(bounds):
        lanes = pl.ds(low_at, size)
        first[k].wait_recv()
        part[:, :, lanes] = (
            wide(x_ref[pl.ds(mine * count, count), :, lanes]) + wide(shard_in[:, :, lanes])
        ).astype(part.dtype)
        second.append(
            [
                send(
                    part.at[target, :, lanes], ctx_in.at[hop, :, lanes],
                    ctx_send.at[hop, k], ctx_recv.at[hop, k], {"ctx": target},
                )
                for hop, target in enumerate(targets)
            ]
        )
    for k, (low_at, size) in enumerate(bounds):
        lanes = pl.ds(low_at, size)
        total = wide(part[place, :, lanes])
        for hop in range(count - 1):
            second[k][hop].wait_recv()
            total = total + wide(ctx_in[hop, :, lanes])
        out_ref[:, lanes] = total
    for k in range(len(bounds)):
        first[k].wait_send()
        for copy in second[k]:
            copy.wait_send()


def scatter_owned(array):
    shard_size, count = lax.axis_size("shard"), lax.axis_size("ctx")
    own, lanes = array.shape[0] // (shard_size * count), array.shape[1]
    if shard_size != 2:
        return lax.psum_scatter(
            array, ("shard", "ctx"), scatter_dimension=0, tiled=True
        ).astype(jnp.float32)
    step = 512
    bounds = [(at, min(step, lanes - at)) for at in range(0, lanes, step)]
    vmem = pl.BlockSpec(memory_space=pltpu.VMEM)

    def kernel(*refs):
        scatter_kernel(bounds, count, *refs)

    parts = len(bounds)
    return pl.pallas_call(
        kernel,
        out_shape=jax.ShapeDtypeStruct((own, lanes), jnp.float32),
        in_specs=[vmem],
        out_specs=vmem,
        scratch_shapes=[
            pltpu.VMEM((count, own, lanes), array.dtype),
            pltpu.VMEM((count, own, lanes), array.dtype),
            pltpu.VMEM((count - 1, own, lanes), array.dtype),
            pltpu.SemaphoreType.DMA((parts,)),
            pltpu.SemaphoreType.DMA((parts,)),
            pltpu.SemaphoreType.DMA((count - 1, parts)),
            pltpu.SemaphoreType.DMA((count - 1, parts)),
        ],
        compiler_params=pltpu.CompilerParams(
            collective_id=1, has_side_effects=True, vmem_limit_bytes=vmem_bytes
        ),
    )(array.reshape(shard_size * count, own, lanes))


def sum_tp(array):
    return lax.psum(array, "tp")


def shards(
    tokens,
    segments,
    gain_one,
    shift_one,
    qkv_weight,
    qv_bias,
    proj_weight,
    proj_bias,
    gain_two,
    shift_two,
    up_weight,
    up_bias,
    down_weight,
    down_bias,
    cotangent,
):
    seq_count, block, width = tokens.shape
    rows = seq_count * block
    own = qkv_weight.shape[0]
    owners = width // own
    heads_dev = qkv_weight.shape[1]
    head_size = qkv_weight.shape[2] // 3
    hidden = up_weight.shape[1]
    mixed_wide = heads_dev * head_size
    scale = head_size ** (-0.5)
    ctx_size = lax.axis_size("ctx")
    ctx_index = lax.axis_index("ctx")
    shard_index = lax.axis_index("shard")
    low = jnp.bfloat16

    small = jnp.concatenate(
        [
            jnp.stack([gain_one, shift_one, proj_bias, gain_two, shift_two, down_bias]),
            columns_of(jnp.concatenate([qv_bias.reshape(-1), up_bias.reshape(-1)]), own),
            columns_of(segments.reshape(-1).astype(low), own),
        ],
        axis=0,
    )
    packed = jnp.concatenate(
        [
            up_weight,
            down_weight.T,
            qkv_weight.reshape(own, -1),
            proj_weight.reshape(mixed_wide, own).T,
            pad_lanes(small.T),
        ],
        axis=1,
    )
    whole = gather_owned(packed)
    at = 0
    up_full = whole[:, at : at + hidden]
    at += hidden
    down_full = whole[:, at : at + hidden]
    at += hidden
    qkv_full = whole[:, at : at + 3 * mixed_wide]
    at += 3 * mixed_wide
    proj_full = whole[:, at : at + mixed_wide]
    at += mixed_wide
    vectors = whole[:, at:].astype(jnp.float32).T
    gain_first, shift_first, bias_proj, gain_second, shift_second, bias_down = (
        vectors[i] for i in range(6)
    )
    by_owner = vectors.reshape(-1, owners, own)
    bias_each = qv_bias.size + up_bias.size
    bias_rows = -(-bias_each // own)
    bias_flat = (
        by_owner[6 : 6 + bias_rows].transpose(1, 0, 2).reshape(owners, -1)[:, :bias_each]
    )
    bias_qv = (
        bias_flat[:, : qv_bias.size]
        .reshape(owners, heads_dev, -1)
        .transpose(1, 0, 2)
        .reshape(heads_dev, 2 * head_size)
    )
    bias_up = (
        bias_flat[:, qv_bias.size :]
        .reshape(owners, up_bias.shape[0], -1)
        .transpose(1, 0, 2)
        .reshape(-1)
    )
    seg_rows = -(-rows // own)
    seg_all = (
        by_owner[6 + bias_rows : 6 + bias_rows + seg_rows]
        .transpose(1, 0, 2)
        .reshape(owners, -1)[:, :rows]
        .astype(jnp.int32)
    )
    seg_k = lax.dynamic_slice_in_dim(seg_all, shard_index * ctx_size, ctx_size, 0).reshape(
        ctx_size, 1, block
    )
    seg_q = jnp.broadcast_to(segments.reshape(block, 1), (block, 128))
    mine = ctx_index.astype(jnp.int32).reshape(1)

    flat = tokens.reshape(rows, width).astype(jnp.float32)
    norm_first, pull_first = jax.vjp(layer_norm, flat, gain_first, shift_first)
    input_low = norm_first.astype(low)
    projected = jnp.dot(input_low, qkv_full, preferred_element_type=jnp.float32).reshape(
        rows, heads_dev, 3 * head_size
    )
    keys_bias = jnp.concatenate(
        [jnp.zeros((heads_dev, head_size), jnp.float32), bias_qv[:, head_size:]], axis=1
    )
    pair_own = (projected[:, :, head_size:] + keys_bias).astype(low)
    query = (projected[:, :, :head_size] + bias_qv[:, :head_size]).astype(low)
    zero_half = jnp.zeros((rows, heads_dev, head_size), low)
    query_pad = jnp.concatenate([query * low(scale), zero_half], axis=2).reshape(
        rows, 2 * mixed_wide
    )
    pairs = lax.all_gather(pair_own.reshape(rows, 2 * mixed_wide), "ctx", axis=0, tiled=True)
    mixed_pad, lse_wide = attend(head_size, mine, query_pad, pairs, seg_q, seg_k)
    mixed_low = (
        mixed_pad.reshape(rows, heads_dev, 2 * head_size)[:, :, head_size:]
        .reshape(rows, mixed_wide)
        .astype(low)
    )
    branch = sum_tp_direct(outer(mixed_low, proj_full).astype(low)).astype(jnp.float32) + bias_proj
    resid = flat + branch
    norm_second, pull_second = jax.vjp(layer_norm, resid, gain_second, shift_second)
    second_low = norm_second.astype(low)
    pre_act = jnp.dot(second_low, up_full, preferred_element_type=jnp.float32) + bias_up
    active, pull_gelu = jax.vjp(gelu_tanh, pre_act)
    active_low = active.astype(low)
    grad_low = cotangent.reshape(rows, width)
    grad_out = grad_low.astype(jnp.float32)
    act_grad = jnp.dot(grad_low, down_full, preferred_element_type=jnp.float32)
    (pre_grad,) = pull_gelu(act_grad)
    pre_low = pre_grad.astype(low)
    norm_two_grad = sum_tp_direct(outer(pre_low, up_full).astype(low)).astype(jnp.float32)
    layer_out = (
        resid + sum_tp(outer(active_low, down_full).astype(low)).astype(jnp.float32) + bias_down
    )
    resid_part, gain_two_grad, shift_two_grad = pull_second(norm_two_grad)
    resid_grad = grad_out + resid_part
    branch_low = resid_grad.astype(low)
    mixed_grad = (
        jnp.dot(branch_low, proj_full, preferred_element_type=jnp.float32)
        .astype(low)
        .reshape(rows, heads_dev, head_size)
    )
    grad_pad = jnp.concatenate([zero_half, mixed_grad], axis=2).reshape(rows, 2 * mixed_wide)

    up_bias_grad = jnp.sum(pre_low.astype(jnp.float32), axis=0).reshape(up_bias.shape[0], -1)
    up_bias_split = columns_of(
        up_bias_grad.reshape(up_bias.shape[0], owners, -1).transpose(1, 0, 2).reshape(owners, -1),
        own,
    )
    second_small = jnp.concatenate(
        [
            jnp.stack(
                [
                    jnp.sum(grad_out, axis=0),
                    jnp.sum(branch_low.astype(jnp.float32), axis=0),
                    gain_two_grad,
                    shift_two_grad,
                ]
            ),
            up_bias_split.transpose(1, 0, 2).reshape(-1, width),
        ],
        axis=0,
    )
    query_grad, pair_total = attend_back(
        head_size, mine, query_pad, grad_pad, mixed_pad, lse_wide, pairs, seg_q, seg_k
    )
    pair_grad = lax.psum_scatter(pair_total, "ctx", scatter_dimension=0, tiled=True)
    query_part = (query_grad.reshape(rows, heads_dev, 2 * head_size)[:, :, :head_size] * scale).astype(
        low
    )
    proj_low = jnp.concatenate(
        [query_part, pair_grad.reshape(rows, heads_dev, 2 * head_size)], axis=2
    ).reshape(rows, 3 * mixed_wide)
    summed_bias = jnp.sum(proj_low.astype(jnp.float32), axis=0).reshape(heads_dev, 3 * head_size)
    qv_bias_grad = jnp.concatenate(
        [summed_bias[:, :head_size], summed_bias[:, 2 * head_size :]], axis=1
    )
    norm_one_grad = sum_tp_direct(outer(proj_low, qkv_full).astype(low)).astype(jnp.float32)
    input_part, gain_one_grad, shift_one_grad = pull_first(norm_one_grad)
    input_grad = resid_grad + input_part
    qv_split = columns_of(
        qv_bias_grad.reshape(heads_dev, owners, -1).transpose(1, 0, 2).reshape(owners, -1), own
    )
    first_small = jnp.concatenate(
        [jnp.stack([gain_one_grad, shift_one_grad]), qv_split.transpose(1, 0, 2).reshape(-1, width)],
        axis=0,
    )
    small_count = second_small.shape[0]
    pieces = scatter_owned(
        jnp.concatenate(
            [
                inner(second_low, pre_low).astype(low),
                inner(grad_low, active_low).astype(low),
                inner(input_low, proj_low).astype(low),
                inner(branch_low, mixed_low).astype(low),
                pad_lanes(jnp.concatenate([second_small, first_small], axis=0).T.astype(low)),
            ],
            axis=1,
        )
    )
    up_piece = pieces[:, :hidden]
    down_piece = pieces[:, hidden : 2 * hidden].T
    at = 2 * hidden
    qkv_piece = pieces[:, at : at + 3 * mixed_wide].reshape(own, heads_dev, 3 * head_size)
    at += 3 * mixed_wide
    proj_piece = pieces[:, at : at + mixed_wide].T.reshape(heads_dev, head_size, own)
    at += mixed_wide
    second_vectors = pieces[:, at : at + small_count].T
    first_vectors = pieces[:, at + small_count : at + small_count + first_small.shape[0]].T
    up_bias_piece = second_vectors[4:].reshape(-1)[: up_bias.size].reshape(up_bias.shape)
    qv_bias_piece = first_vectors[2:].reshape(-1)[: qv_bias.size].reshape(qv_bias.shape)
    return (
        layer_out.astype(low).reshape(seq_count, block, width),
        input_grad.reshape(seq_count, block, width),
        first_vectors[0],
        first_vectors[1],
        qkv_piece,
        qv_bias_piece,
        proj_piece,
        second_vectors[1],
        second_vectors[2],
        second_vectors[3],
        up_piece,
        up_bias_piece,
        down_piece,
        second_vectors[0],
    )


def solution(mesh):
    placed = (
        P("shard", "ctx", None),
        P("shard", "ctx"),
        P(("shard", "ctx")),
        P(("shard", "ctx")),
        P(("shard", "ctx"), "tp", None),
        P("tp", ("shard", "ctx")),
        P("tp", None, ("shard", "ctx")),
        P(("shard", "ctx")),
        P(("shard", "ctx")),
        P(("shard", "ctx")),
        P(("shard", "ctx"), "tp"),
        P("tp", ("shard", "ctx")),
        P("tp", ("shard", "ctx")),
        P(("shard", "ctx")),
        P("shard", "ctx", None),
    )
    return jax.shard_map(
        shards,
        mesh=mesh,
        in_specs=placed,
        out_specs=(
            P("shard", "ctx", None),
            P("shard", "ctx", None),
            P(("shard", "ctx")),
            P(("shard", "ctx")),
            P(("shard", "ctx"), "tp", None),
            P("tp", ("shard", "ctx")),
            P("tp", None, ("shard", "ctx")),
            P(("shard", "ctx")),
            P(("shard", "ctx")),
            P(("shard", "ctx")),
            P(("shard", "ctx"), "tp"),
            P("tp", ("shard", "ctx")),
            P("tp", ("shard", "ctx")),
            P(("shard", "ctx")),
        ),
        check_vma=False,
    )
```
